32 devices in a mesh: yslab: 4 (over x, core), zblock: 8 (over z, y).
Axes of the slice: x: 2, y: 2, z: 4, core: 2. Of those that a mesh axis runs over, the one named last changes fastest.
Arguments:
- volume: float32 [512, 512, 512], P('yslab', 'zblock'), may hold values from -6 to 6
- shift_x: int32 [2, 512], replicated, may hold values from -11584 to 11584, as said below
- shift_z: int32 [2, 512], replicated, may hold values from -11584 to 11584, as said below
- mask: int32 [2, 512, 512], P(None, 'yslab', 'zblock'), may hold values from 0 to 1, as said below
- measured: float32 [2, 2, 512, 512], P(None, None, 'yslab', 'zblock'), may hold values from -6 to 6
Outputs:
- corrected: float32 [2, 2, 512, 512], P(None, None, 'yslab', 'zblock')
The draws below stay inside these ranges and needn't reach their ends.
Inputs may be any that keep to these rules, and one draw needn't show every extreme that they name: shift_x holds shifts in units of 1/64 of a cell. shift_z holds shifts in units of 1/64 of a cell. mask[t] is 1 exactly where |q_y(h)| * 512 * a_t <= |q_x(k)| * 512 * b_t with signed frequencies and integers a_t, b_t of 1 to 3, else 0.
All inputs are finite; a program needn't handle non-finite values.
Results may differ from the reference program's by a relative error of at most 0.0001.
Values sent between devices are 32-bit elements; how exact they have to be, the bound alone decides.
A program may use at most 192 MiB of HBM per device.

```python
import math
import jax
import jax.numpy as jnp
from jax import lax

NX = 512
NZ = 512
TILTS = 2
SUB = 64
NY = 512


def draw_line_shifts(key, length, salt):
    drawn = jax.random.randint(jax.random.fold_in(key, salt), (TILTS, 1), -45, 46)
    flip = jax.random.randint(jax.random.fold_in(key, salt + 2), (1, 1), 0, 2) * 2 - 1
    tilt_index = jnp.arange(TILTS, dtype=jnp.int32)[:, None]
    alternate = jnp.where(jnp.mod(tilt_index, 2) == 0, 1, -1) * flip * 45
    slope = jnp.where(tilt_index < 2, alternate, drawn)
    jitter = jax.random.randint(jax.random.fold_in(key, salt + 1), (TILTS, length), -64, 65)
    first_col = jnp.arange(length, dtype=jnp.int32)[None, :] == 0
    edge = jnp.where(slope > 0, -64, 64)
    jitter = jnp.where(first_col, edge, jitter)
    place = jnp.arange(length, dtype=jnp.int32) - length // 2
    return (slope * place[None, :] + jitter).astype(jnp.int32)


def draw_shift_x(key, part):
    return draw_line_shifts(key, NZ, 11)


def draw_shift_z(key, part):
    return draw_line_shifts(key, NX, 23)


def draw_mask(key, part):
    steep = jax.random.randint(jax.random.fold_in(key, 37), (TILTS, 1, 1), 1, 4)
    flat = jax.random.randint(jax.random.fold_in(key, 41), (TILTS, 1, 1), 1, 4)
    rows_freq = jnp.arange(NY, dtype=jnp.int32)
    cols_freq = jnp.arange(NX, dtype=jnp.int32)
    rows_signed = jnp.abs(jnp.mod(rows_freq + NY // 2, NY) - NY // 2)
    cols_signed = jnp.abs(jnp.mod(cols_freq + NX // 2, NX) - NX // 2)
    inside = rows_signed[None, :, None] * NX * steep <= cols_signed[None, None, :] * NY * flat
    return jnp.where(inside, 1, 0).astype(jnp.int32)


def block_scale(rng, extent, cuts, least, largest):
    loudness = 1.0
    for position, blocks in cuts:
        heights = jax.random.uniform(jax.random.fold_in(jax.random.fold_in(rng, 6), position), (blocks,), jnp.float32, least / len(cuts), largest / len(cuts))
        loudness = loudness * jnp.repeat(jnp.exp(heights), extent[position] // blocks).reshape((-1,) + (1,) * (len(extent) - 1 - position))
    return loudness


def scatter_about(own_key, extent, scale, most, cuts=(), kind=jnp.bfloat16):
    level = block_scale(own_key, extent, cuts, -0.22, 0.18) if cuts else 1.0
    values = jax.random.normal(own_key, extent, jnp.float32) * scale * level
    return jnp.minimum(jnp.maximum(values, -most), most).astype(kind)


def setup_inputs(seed: int = 0) -> dict:
    arg_keys = jax.random.split(jax.random.key(seed), 6)
    volume = scatter_about(arg_keys[0], (NY, NZ, NX), 1.0, 6.0, ((0, 4), (1, 8)), jnp.float32)
    shift_x = draw_shift_x(jax.random.fold_in(arg_keys[5], 71), 0)
    shift_z = draw_shift_z(jax.random.fold_in(arg_keys[5], 71), 0)
    mask = draw_mask(jax.random.fold_in(arg_keys[5], 71), 0)
    measured = scatter_about(arg_keys[4], (2, TILTS, NY, NX), 1.0, 6.0, ((2, 4), (3, 8)), jnp.float32)
    return {"volume": volume, "shift_x": shift_x, "shift_z": shift_z, "mask": mask, "measured": measured}


def ramp_pair(shifts, length):
    freq = jnp.arange(length, dtype=jnp.int32)
    signed = jnp.mod(freq + length // 2, length) - length // 2
    turns = jnp.mod(shifts[..., None] * signed, SUB * length).astype(jnp.float32)
    angle = 2.0 * math.pi / (SUB * length) * turns
    return (jnp.cos(angle), jnp.sin(angle))

def reference(volume, shift_x, shift_z, mask, measured):
    results = []
    volume_spec = jnp.fft.fft(volume, axis=2)
    for tilt in range(TILTS):
        cos_x, sin_x = ramp_pair(shift_x[tilt], NX)
        phase_x = cos_x - 1j * sin_x
        first = jnp.real(jnp.fft.ifft(volume_spec * phase_x[None], axis=2))
        cos_z, sin_z = ramp_pair(shift_z[tilt], NZ)
        phase_z = jnp.transpose(cos_z - 1j * sin_z)
        second = jnp.real(jnp.fft.ifft(jnp.fft.fft(first, axis=1) * phase_z[None], axis=1))
        third = jnp.fft.fft(second, axis=2) * phase_x[None]
        line = lax.optimization_barrier(jnp.sum(third, axis=1)) / math.sqrt(NZ * NX)
        results.append(jnp.fft.fft(line, axis=0) / math.sqrt(NY))
    spectrum = jnp.stack(results)
    spectrum = jnp.stack([jnp.real(spectrum), jnp.imag(spectrum)]).astype(jnp.float32)
    weight = mask.astype(jnp.float32)[None]
    return spectrum + weight * (measured - spectrum)
```

```python
import functools
import math

import jax
import jax.numpy as jnp
import ml_dtypes
import numpy as np
from jax import lax
from jax.experimental import pallas as pl
from jax.experimental.pallas import tpu as pltpu
from jax.sharding import PartitionSpec as P

SUB = 64
HIGH = lax.Precision.HIGHEST
F32 = jnp.float32
BF16 = jnp.bfloat16


def ramp_pair(shifts, freq, length):
    turns = jnp.mod(shifts[..., None] * freq, SUB * length).astype(F32)
    angle = 2.0 * math.pi / (SUB * length) * turns
    return jnp.cos(angle), jnp.sin(angle)


def split3(weights):
    lead = lax.reduce_precision(weights, 8, 7)
    rest = lax.reduce_precision(weights - lead, 8, 7)
    return jnp.concatenate([lead, rest, lead], axis=-2).astype(BF16)


def fixed_split3(weights):
    lead = weights.astype(np.float32).astype(ml_dtypes.bfloat16)
    rest = (weights - lead.astype(np.float32)).astype(ml_dtypes.bfloat16)
    return jnp.asarray(np.concatenate([lead, rest, lead], axis=0))


def parts(values):
    lead = values.astype(BF16)
    return lead, (values - lead.astype(F32)).astype(BF16)


def triple(values, stacked):
    lead, rest = parts(values)
    return jnp.dot(
        jnp.concatenate([lead, lead, rest], axis=1), stacked, preferred_element_type=F32
    )


def half_waves(length):
    half, quarter = length // 2, length // 4
    place = np.arange(half)
    even, odd = 2 * np.arange(quarter), 2 * np.arange(quarter) + 1

    def waves(freq):
        turn = 2.0 * np.pi * ((place[:, None] * freq[None, :]) % length) / length
        return np.cos(turn), np.sin(turn)

    ec, es = waves(even)
    oc, os_ = waves(odd)
    sign = np.where(place % 2 == 0, 1.0, -1.0)
    es[:, 0] = sign
    forward_even = np.concatenate([ec, es], axis=1)
    forward_odd = np.concatenate([oc, os_], axis=1)
    gain = np.full((length // 2,), 2.0 / length)
    back_odd = (forward_odd * gain).T
    gain_even = gain.copy()
    gain_even[0] = 1.0 / length
    gain_even[quarter] = 1.0 / length
    back_even = (forward_even * gain_even).T
    return [m.astype(np.float32) for m in (forward_even, forward_odd, back_even, back_odd)]


def depth_waves(length):
    half = length // 2
    n = np.arange(half)
    turn = 2.0 * np.pi * ((n[:, None] * np.arange(length)[None, :]) % length) / length
    cos, sin = np.cos(turn) * 2.0 / length, np.sin(turn) * 2.0 / length
    cos[0] = 1.0 / length
    sin[0] = np.where(np.arange(length) % 2 == 0, 1.0, -1.0) / length
    return np.concatenate([cos, sin], axis=0).astype(np.float32)


def line_kernel(
    tilts, v_ref, row_ref, turn_ref, spread_ref, wave_ref, fe_ref, fo_ref, be_ref, bo_ref,
    acc_ref, sum_ref,
):
    @pl.when(pl.program_id(0) == 0)
    def _():
        acc_ref[...] = jnp.zeros_like(acc_ref)
        sum_ref[...] = jnp.zeros_like(sum_ref)

    half = v_ref.shape[2] // 2
    quarter = half // 2
    values = v_ref[0]
    near, far = values[:, :half], values[:, half:]
    even = triple(near + far, fe_ref[...])
    odd = triple(near - far, fo_ref[...])
    sum_ref[...] += even[:, :quarter]
    row = row_ref[0]
    depth_cos, depth_cos_b, depth_sin = row[0:1], row[1:2], row[2:3]
    for tilt in range(tilts):
        base = 3 + 3 * tilt
        cos_a, cos_b, sin = row[base : base + 1], row[base + 1 : base + 2], row[base + 2 : base + 3]

        def turned(spec, lanes):
            re, im = spec[:, :quarter], spec[:, quarter:]
            s = sin[:, lanes]
            return jnp.concatenate(
                [re * cos_a[:, lanes] - im * s, im * cos_b[:, lanes] + re * s], axis=1
            )

        back_even = triple(turned(even, slice(0, quarter)), be_ref[...])
        back_odd = triple(turned(odd, slice(quarter, half)), bo_ref[...])
        total = None
        for block, first in enumerate((back_even + back_odd, back_even - back_odd)):
            rows = slice(block * half, (block + 1) * half)
            c, s = turn_ref[tilt, rows, :half], turn_ref[tilt, rows, half:]
            mixed = jnp.concatenate(
                [c * depth_cos - s * depth_sin, s * depth_cos_b + c * depth_sin], axis=1
            )
            spread = triple(mixed, spread_ref[tilt])
            re, im = spread[:, :half], spread[:, half:]
            wc, ws = wave_ref[rows, :half], wave_ref[rows, half:]
            kernel = jnp.concatenate([re * wc + im * ws, im * wc - re * ws], axis=1)
            lead, rest = parts(kernel)
            a, b = parts(first)
            part = jnp.dot(
                jnp.concatenate([a, a, b], axis=1),
                jnp.concatenate([lead, rest, lead], axis=0),
                preferred_element_type=F32,
            )
            total = part if total is None else total + part
        acc_ref[tilt] += total


def lines(volume, rows, turn, spread, wave, weights):
    depth, ydev, width = volume.shape
    tilts = turn.shape[0]
    whole = lambda x: pl.BlockSpec(x.shape, lambda z: (0,) * x.ndim)
    flops = 2 * 3 * depth * width * width * (ydev // 2 + tilts * (ydev // 2 + width + ydev))
    return pl.pallas_call(
        functools.partial(line_kernel, tilts),
        grid=(depth,),
        in_specs=[
            pl.BlockSpec((1, ydev, width), lambda z: (z, 0, 0)),
            pl.BlockSpec((1,) + rows.shape[1:], lambda z: (z, 0, 0)),
            whole(turn), whole(spread), whole(wave),
        ] + [whole(w) for w in weights],
        out_specs=[
            pl.BlockSpec((tilts, ydev, width), lambda z: (0, 0, 0)),
            pl.BlockSpec((ydev, width // 4), lambda z: (0, 0)),
        ],
        out_shape=[
            jax.ShapeDtypeStruct((tilts, ydev, width), F32),
            jax.ShapeDtypeStruct((ydev, width // 4), F32),
        ],
        compiler_params=pltpu.CompilerParams(vmem_limit_bytes=56 * 2**20),
        cost_estimate=pl.CostEstimate(
            flops=flops, bytes_accessed=volume.size * 4, transcendentals=0
        ),
    )(volume, rows, turn, spread, wave, *weights)


def on_device(volume, shift_x, shift_z, mask, measured):
    zparts = lax.axis_size("zblock")
    yparts = lax.axis_size("yslab")
    zindex = lax.axis_index("zblock")
    yindex = lax.axis_index("yslab")
    ydev, zdev, width = volume.shape
    depth = zdev * zparts
    rows_all = ydev * yparts
    tilts = shift_x.shape[0]
    half = width // 2
    share = zdev // 2
    core = lax.rem(yindex, 2)

    keep = lax.dynamic_slice_in_dim(volume, core * share, share, 1)
    give = lax.dynamic_slice_in_dim(volume, (1 - core) * share, share, 1)
    taken = lax.ppermute(give, "yslab", [(i, i ^ 1) for i in range(yparts)])
    mine = jnp.concatenate([jnp.transpose(keep, (1, 0, 2)), jnp.transpose(taken, (1, 0, 2))], 1)

    zplace = zindex * zdev + core * share + jnp.arange(share, dtype=jnp.int32)
    n = np.arange(half, dtype=np.int32)
    zc, zs = ramp_pair(zplace * SUB, n, depth)
    flip = (1 - 2 * jnp.mod(zplace, 2)).astype(F32)
    zc_b = jnp.where(n[None, :] == 0, flip[:, None], zc)
    folded = np.concatenate([n[0::2], n[1::2]])
    local = lax.dynamic_slice_in_dim(shift_x, zplace[0], share, 1)
    xc, xs = ramp_pair(local, folded, width)
    xn, _ = ramp_pair(local, np.full((1,), half, np.int32), width)
    xc_b = jnp.where(folded == 0, xn, xc)
    stack = [zc, zc_b, zs]
    for tilt in range(tilts):
        stack += [xc[tilt], xc_b[tilt], xs[tilt]]
    rows = jnp.stack(stack, axis=1)
    rows = jnp.pad(rows, ((0, 0), (0, -rows.shape[1] % 8), (0, 0)))

    tc, ts = ramp_pair(shift_z, n, depth)
    tn, _ = ramp_pair(shift_z, np.full((1,), half, np.int32), depth)
    turn = jnp.concatenate([tc, jnp.where(n == 0, tn, ts)], axis=2)

    k = n.copy()
    k[0] = -half
    wc, ws = ramp_pair(shift_x, k, width)
    scale = 1.0 / math.sqrt(depth * width) / math.sqrt(rows_all)
    third = jnp.concatenate([wc, -ws], axis=2) * scale
    spread = split3(jnp.einsum("cz,tzk->tck", depth_waves(depth), third, precision=HIGH))

    angle = 2.0 * np.pi * ((np.arange(width)[:, None] * k[None, :]) % width) / width
    wave = np.concatenate([np.cos(angle), np.sin(angle)], axis=1).astype(np.float32)
    wave[:, half] = 0.0
    weights = [fixed_split3(m) for m in half_waves(width)]

    acc, sums = lines(mine, rows, turn, spread, jnp.asarray(wave), weights)

    re, im = acc[:, :, :half], acc[:, :, half:]
    zero_re = jnp.broadcast_to((sums[:, :1] * scale)[None], (tilts,) + sums[:, :1].shape)
    line_re = jnp.concatenate([zero_re, re[:, :, 1:], re[:, :, :1], re[:, :, :0:-1]], axis=2)
    line_im = jnp.concatenate(
        [jnp.zeros_like(zero_re), im[:, :, 1:], im[:, :, :1], -im[:, :, :0:-1]], axis=2
    )
    line = lax.psum_scatter(
        jnp.stack([line_re, line_im]), "zblock", scatter_dimension=3, tiled=True
    )

    low, other = ydev * yindex, ydev * (yindex + 1 - 2 * core)
    place = jnp.concatenate(
        [low + jnp.arange(ydev, dtype=jnp.int32), other + jnp.arange(ydev, dtype=jnp.int32)]
    )
    h = jnp.arange(rows_all, dtype=jnp.int32)
    turns = jnp.mod(h[:, None] * place[None, :], rows_all).astype(F32)
    hc, hs = jnp.cos(2.0 * math.pi / rows_all * turns), jnp.sin(2.0 * math.pi / rows_all * turns)
    across = jnp.concatenate(
        [jnp.concatenate([hc, hs], axis=1), jnp.concatenate([-hs, hc], axis=1)], axis=0
    )
    line = jnp.transpose(line, (0, 2, 1, 3)).reshape(4 * ydev, -1)
    term = jnp.dot(across, line, precision=HIGH).reshape(2, rows_all, tilts, -1)
    gathered = lax.psum_scatter(term, "yslab", scatter_dimension=1, tiled=True)
    spectrum = jnp.transpose(gathered, (0, 2, 1, 3))
    weight = mask.astype(F32)[None]
    return spectrum + weight * (measured - spectrum)


def solution(mesh):
    in_specs = (
        P("yslab", "zblock", None),
        P(),
        P(),
        P(None, "yslab", "zblock"),
        P(None, None, "yslab", "zblock"),
    )
    out_specs = P(None, None, "yslab", "zblock")
    return jax.shard_map(
        on_device, mesh=mesh, in_specs=in_specs, out_specs=out_specs, check_vma=False
    )
```
